32 devices in a mesh: groups: 2 (over y), row: 4 (over x, core), col: 4 (over z).
Axes of the slice: x: 2, y: 2, z: 4, core: 2. Of those that a mesh axis runs over, the one named last changes fastest.
Arguments:
- pair_map: bfloat16 [192, 96, 128], P(('groups', 'row'), 'col'), parts along dimension 0, may hold values from -6 to 6
- cotangent: bfloat16 [192, 96, 128], P(('groups', 'row'), 'col'), parts along dimension 0, may hold values from -6 to 6
- residue_mask: int32 [192], P('groups'), parts along dimension 0, may hold values from 0 to 1, as said below
- gain_in: float32 [128], replicated, may hold values from 0.25 to 1.75
- w_in: bfloat16 [128, 640], replicated, may hold values from -0.5 to 0.5
- gain_mid: float32 [128], replicated, may hold values from 0.25 to 1.75
- w_out: bfloat16 [128, 128], replicated, may hold values from -0.5 to 0.5
- gain_trans: float32 [128], replicated, may hold values from 0.25 to 1.75
- w_up: bfloat16 [128, 512], replicated, may hold values from -0.5 to 0.5
- w_down: bfloat16 [512, 128], replicated, may hold values from -0.25 to 0.25
Outputs:
- updated: bfloat16 [192, 96, 128], P(('groups', 'row'), 'col'), parts along dimension 0
- gradient: bfloat16 [192, 96, 128], P(('groups', 'row'), 'col'), parts along dimension 0
The draws below stay inside these ranges and needn't reach their ends.
There are 2 independent parts, one for each index of `groups`. The reference program is written for one: setup_inputs(seed, part) draws one part's arguments, and reference() takes and returns one part's arrays. A program takes and returns all parts, laid end to end along the dimension named above; an argument that names none is the same for every part. Nothing has to cross between parts.
Inputs may be any that keep to these rules, and one draw needn't show every extreme that they name: `residue_mask`: the complex is 4 slots of 24 residues each; in every slot the present residues come first, at least 3/5 of the slot (rounded down) and never the whole slot.
All inputs are finite; a program needn't handle non-finite values.
Results may differ from the reference program's by a relative error of at most 0.019.
The reference program's roundings to bfloat16 on the way count: a program that leaves them out, or rounds other values in their place, can miss the bound.
Values may be sent and summed in bfloat16 or wider, within the bound.
A program may use at most 64 MiB of HBM per device.

```python
import jax
import jax.numpy as jnp
from jax import lax

C = 128
H = 128
FF = 512
CHAINS = 4
N = 96


def draw_residue_mask(key, part):
    key = jax.random.fold_in(key, 11)
    slot_size = N // CHAINS
    lengths = jax.random.randint(key, (CHAINS,), 3 * slot_size // 5, slot_size)
    position = jnp.arange(N) % slot_size
    chain_index = jnp.arange(N) // slot_size
    return (position < lengths[chain_index]).astype(jnp.int32)


def block_scale(stream_key, dims, split, smallest, largest):
    loudness = 1.0
    for axis_at, shards_of in split:
        heights = jax.random.uniform(jax.random.fold_in(jax.random.fold_in(stream_key, 6), axis_at), (shards_of,), jnp.float32, smallest / len(split), largest / len(split))
        loudness = loudness * jnp.repeat(jnp.exp(heights), dims[axis_at] // shards_of).reshape((-1,) + (1,) * (len(dims) - 1 - axis_at))
    return loudness


def gaussian(rng, shape, deviation, most, cuts=(), dtype=jnp.bfloat16):
    factor_of = block_scale(rng, shape, cuts, -0.22, 0.18) if cuts else 1.0
    array = jax.random.normal(rng, shape, jnp.float32) * deviation * factor_of
    return jnp.minimum(jnp.maximum(array, -most), most).astype(dtype)


def setup_inputs(seed: int = 0, part: int = 0) -> dict:
    keys = jax.random.split(jax.random.key(seed), 11)
    part_splits = jax.random.split(jax.random.fold_in(keys[10], part), 11)
    pair_map = gaussian(part_splits[0], (N, N, C), 1.0, 6.0, ((0, 4), (1, 4)))
    cotangent = gaussian(part_splits[1], (N, N, C), 1.0, 6.0, ((0, 4), (1, 4)))
    residue_mask = draw_residue_mask(jax.random.fold_in(jax.random.fold_in(keys[10], part), 71), part)
    gain_in = jnp.clip(1.0 + 0.15 * jax.random.normal(keys[3], (C,), jnp.float32), 0.25, 1.75)
    w_in = gaussian(keys[4], (C, 4 * H + C), C ** -0.5, 0.5)
    gain_mid = jnp.clip(1.0 + 0.15 * jax.random.normal(keys[5], (H,), jnp.float32), 0.25, 1.75)
    w_out = gaussian(keys[6], (H, C), H ** -0.5, 0.5)
    gain_trans = jnp.clip(1.0 + 0.15 * jax.random.normal(keys[7], (C,), jnp.float32), 0.25, 1.75)
    w_up = gaussian(keys[8], (C, FF), C ** -0.5, 0.5)
    w_down = gaussian(keys[9], (FF, C), FF ** -0.5, 0.25)
    return {"pair_map": pair_map, "cotangent": cotangent, "residue_mask": residue_mask, "gain_in": gain_in, "w_in": w_in, "gain_mid": gain_mid, "w_out": w_out, "gain_trans": gain_trans, "w_up": w_up, "w_down": w_down}


epsilon = 1e-05

def layer_norm(values, gain_vec):
    centred = values - lax.optimization_barrier(jnp.mean(values, axis=-1, keepdims=True))
    spread = lax.optimization_barrier(jnp.mean(centred * centred, axis=-1, keepdims=True))
    return centred * lax.rsqrt(spread + epsilon) * gain_vec

def project_in(pair_vals, row_mask, col_mask, gain_in, w_in):
    inner_width = (w_in.shape[1] - pair_vals.shape[-1]) // 4
    normed = layer_norm(pair_vals, gain_in).astype(jnp.bfloat16)
    projected = jnp.dot(normed, w_in, preferred_element_type=jnp.float32)
    pair_mask = row_mask[:, None, None] * col_mask[None, :, None]
    left_proj = pair_mask * jax.nn.sigmoid(projected[..., inner_width:2 * inner_width]) * projected[..., :inner_width]
    right_proj = pair_mask * jax.nn.sigmoid(projected[..., 3 * inner_width:4 * inner_width]) * projected[..., 2 * inner_width:3 * inner_width]
    gate_vals = jax.nn.sigmoid(projected[..., 4 * inner_width:])
    return (left_proj, right_proj, gate_vals)

def project_out(combined, gate_vals, pair_vals, gain_mid, w_out):
    mixed_norm = layer_norm(combined, gain_mid).astype(jnp.bfloat16)
    return pair_vals + gate_vals * jnp.dot(mixed_norm, w_out, preferred_element_type=jnp.float32)

def transition(carried, gain_trans, w_up, w_down):
    lifted = layer_norm(carried, gain_trans).astype(jnp.bfloat16)
    hidden_units = jax.nn.relu(jnp.dot(lifted, w_up, preferred_element_type=jnp.float32)).astype(jnp.bfloat16)
    return carried + jnp.dot(hidden_units, w_down, preferred_element_type=jnp.float32)

def reference(pair_map, cotangent, residue_mask, gain_in, w_in, gain_mid, w_out, gain_trans, w_up, w_down):
    present = residue_mask.astype(jnp.float32)
    pair_vals = pair_map.astype(jnp.float32)

    def project_entry(values):
        return project_in(values, present, present, gain_in, w_in)
    (left_proj, right_proj, gate_vals), entry_back = jax.vjp(project_entry, pair_vals)
    left_half = left_proj.astype(jnp.bfloat16)
    right_half = right_proj.astype(jnp.bfloat16)
    combined = jnp.einsum('ikh,jkh->ijh', left_half.astype(jnp.float32), right_half.astype(jnp.float32))

    def project_exit(comb_in, gate_in, values):
        return project_out(comb_in, gate_in, values, gain_mid, w_out)
    sectioned, exit_back = jax.vjp(project_exit, combined, gate_vals, pair_vals)
    carried = lax.optimization_barrier(sectioned.astype(jnp.bfloat16)).astype(jnp.float32)

    def transition_step(values):
        return transition(values, gain_trans, w_up, w_down)
    result, step_back = jax.vjp(transition_step, carried)
    updated = result.astype(jnp.bfloat16)
    d_carried, = step_back(cotangent.astype(jnp.float32))
    d_combined, d_gate, d_direct = exit_back(d_carried)
    d_comb_f = lax.optimization_barrier(d_combined.astype(jnp.bfloat16)).astype(jnp.float32)
    d_left = jnp.einsum('ijh,jkh->ikh', d_comb_f, right_half.astype(jnp.float32))
    d_right = jnp.einsum('ijh,ikh->jkh', d_comb_f, left_half.astype(jnp.float32))
    d_entry, = entry_back((d_left, d_right, d_gate))
    return (updated, (d_entry + d_direct).astype(jnp.bfloat16))
```

```python
import functools

import jax
import jax.numpy as jnp
from jax import lax
from jax.experimental import pallas as pl
from jax.experimental.pallas import tpu as pltpu
from jax.sharding import PartitionSpec as P

epsilon = 1e-05
PIECES = 4
MESH = pl.DeviceIdType.MESH
F32 = jnp.float32
BF16 = jnp.bfloat16


def nn(a, b):
    return jnp.dot(a, b, preferred_element_type=F32)


def nt(a, b):
    return lax.dot_general(a, b, (((1,), (1,)), ((), ())), preferred_element_type=F32)


def ln(values):
    centred = values - jnp.mean(values, axis=-1, keepdims=True)
    inv = lax.rsqrt(jnp.mean(centred * centred, axis=-1, keepdims=True) + epsilon)
    return centred * inv, inv


def ln_back(d_hat, hat, inv):
    return inv * (
        d_hat
        - jnp.mean(d_hat, axis=-1, keepdims=True)
        - hat * jnp.mean(d_hat * hat, axis=-1, keepdims=True)
    )


def sigmoid(v):
    return jax.nn.sigmoid(v)


def products(t, a_ref, a_row, b_ref, b_rows, out_ref, add):
    def block(n, _):
        acc = [None] * 8
        for s in range(t):
            b = b_ref[b_rows(s), :]
            for u in range(8):
                term = a_ref[pl.ds(a_row(n * 8 + u, s), 1), :] * b
                acc[u] = term if acc[u] is None else acc[u] + term
        for u in range(8):
            at = pl.ds(pl.multiple_of((n * 8 + u) * t, 8), t)
            out_ref[at, :] = out_ref[at, :] + acc[u] if add else acc[u]
        return 0

    lax.fori_loop(0, t // 8, block, 0)


def kernel(
    peers, t, step,
    mask_ref, x_ref, cot_ref, gin_ref, win_ref, gmid_ref, wout_ref, gtr_ref, wup_ref, wdn_ref,
    up_ref, grad_ref,
    r_all, l_all, rt, l_row, dc_row, dc_col,
    mask_v, hat_v, inv_v, proj_v, own_v, a_v, b_v, dleft_v, dright_v, dcar_v, dgate_v,
    s_send, s_recv,
):
    row, col = lax.axis_index("row"), lax.axis_index("col")
    rows = t * t
    c = x_ref.shape[-1]
    chunks = [pl.ds(n, step) for n in range(0, rows, step)]

    barrier = pltpu.get_barrier_semaphore()
    for s in range(1, peers):
        pl.semaphore_signal(
            barrier, inc=1, device_id={"row": lax.rem(row + s, peers)}, device_id_type=MESH
        )
        pl.semaphore_signal(
            barrier, inc=1, device_id={"col": lax.rem(col + s, peers)}, device_id_type=MESH
        )

    def copy(kind, src, dst, slot, axis, peer, lane=None):
        return pltpu.make_async_remote_copy(
            src_ref=src, dst_ref=dst,
            send_sem=s_send.at[kind if lane is None else lane, peer if lane is None else slot],
            recv_sem=s_recv.at[kind, slot], device_id={axis: peer}, device_id_type=MESH,
        )

    size = rows // PIECES
    mine = lax.rem(row, PIECES)
    base = row - mine

    def part(ref, slot, p):
        return ref.at[slot, pl.ds(pl.multiple_of(p * size, 16), size)]

    def first(src, peer, p):
        return copy(0, part(r_all, src, p), part(r_all, src, p), src, "row", peer)

    def left_over_rows(src, peer):
        return copy(1, l_all.at[src], l_all.at[src], src, "row", peer)

    def to_column(src, slot, peer):
        return copy(2, part(r_all, src, mine), part(rt, slot, mine), slot, "col", peer)

    def in_set(slot, m, p, peer):
        d = part(rt, slot, p)
        return copy(2 + m, d, d, slot, "row", peer, lane=2 + m)

    def rest(src, m, p, peer):
        d = part(r_all, src, p)
        return copy(5 + m, d, d, src, "row", peer)

    def dc_over_rows(src, slot, peer):
        return copy(9, dc_row.at[src], dc_col.at[slot], slot, "row", peer)

    def along(kind, ref, tile, n, up):
        d = ref.at[tile, chunks[n]]
        peer = col + 1 if up else col - 1
        return copy(kind + n, d, d, tile, "col", peer, lane=kind + n + (0 if up else 6))

    def pass_on(kind, ref, tile, n, up):
        @pl.when((col + 1 < peers) if up else (col > 0))
        def _():
            along(kind, ref, tile, n, up).start()

    def forward(kind, ref, s):
        for n in range(len(chunks)):
            for up in (True, False):
                tile = col - s if up else col + s

                @pl.when((tile >= 0) if up else (tile < peers))
                def _():
                    along(kind, ref, tile, n, not up).wait_recv()
                    pass_on(kind, ref, tile, n, up)

    def both(s, body):
        @pl.when(col - s >= 0)
        def _():
            body(col - s)

        @pl.when(col + s < peers)
        def _():
            body(col + s)

    def start_rest():
        def per_peer(s, _):
            peer = lax.rem(row + s, peers)
            for m in range(1, PIECES):
                rest(row, m, lax.rem(lax.rem(peer, PIECES) + m, PIECES), peer).start()
            return 0

        lax.fori_loop(1, peers, per_peer, 0)

    def wait_rest(src):
        for m in range(1, PIECES):
            rest(src, m, lax.rem(mine + m, PIECES), src).wait_recv()

    at_k = lax.broadcasted_iota(jnp.int32, (t, c), 0)
    m_k = jnp.zeros((t, c), F32)
    for k in range(t):
        m_k = jnp.where(at_k == k, mask_ref[col * t + k].astype(F32), m_k)
    for i in range(t):
        mask_v[i * t : (i + 1) * t, :] = m_k * mask_ref[row * t + i].astype(F32)

    for at in chunks:
        hat, inv = ln(x_ref[at, :].astype(F32))
        hat_v[at, :] = hat
        inv_v[at, :] = jnp.broadcast_to(inv, hat.shape)
        normed = (hat * gin_ref[...]).astype(BF16)
        pr = nn(normed, win_ref[:, 2 * c : 4 * c])
        gate = sigmoid(pr[:, c:])
        proj_v[at, 2 * c : 3 * c] = pr[:, :c]
        proj_v[at, 3 * c : 4 * c] = gate
        r_all[row, at, :] = (mask_v[at, :] * gate * pr[:, :c]).astype(BF16)

    pl.semaphore_wait(barrier, 2 * (peers - 1))

    def send_r(s, _):
        peer = lax.rem(row + s, peers)
        first(row, peer, lax.rem(peer, PIECES)).start()
        return 0

    lax.fori_loop(1, peers, send_r, 0)

    for n, at in enumerate(chunks):
        normed = (hat_v[at, :] * gin_ref[...]).astype(BF16)
        pr = nn(normed, win_ref[:, : 2 * c])
        gate = sigmoid(pr[:, c:])
        proj_v[at, :c] = pr[:, :c]
        proj_v[at, c : 2 * c] = gate
        left = (mask_v[at, :] * gate * pr[:, :c]).astype(BF16)
        l_row[col, at, :] = left
        for up in (True, False):
            pass_on(10, l_row, col, n, up)
        l_all[row, at, :] = left

    def piece_step(s, _):
        src = lax.rem(row - s + peers, peers)

        @pl.when(s > 0)
        def _():
            first(src, src, mine).wait_recv()

        @pl.when(src != col)
        def _():
            to_column(src, col, src).start()

        return 0

    lax.fori_loop(0, peers, piece_step, 0)

    @pl.when(row == col)
    def _():
        start_rest()

    for at in chunks:
        normed = (hat_v[at, :] * gin_ref[...]).astype(BF16)
        proj_v[at, 4 * c :] = sigmoid(nn(normed, win_ref[:, 4 * c :]))
        own_v[at, :] = jnp.zeros((step, c), F32)

    def share(slot):
        to_column(slot, slot, slot).wait_recv()
        for m in range(1, PIECES):
            in_set(slot, m, mine, base + lax.rem(mine + m, PIECES)).start()

    def combine(slot):
        @pl.when(slot == col)
        def _():
            @pl.when(row != col)
            def _():
                wait_rest(col)

            for at in chunks:
                b_v[at, :] = r_all[col, at, :].astype(F32)

        @pl.when(slot != col)
        def _():
            for m in range(1, PIECES):
                p = lax.rem(mine - m + PIECES, PIECES)
                in_set(slot, m, p, base + p).wait_recv()
            for at in chunks:
                b_v[at, :] = rt[slot, at, :].astype(F32)

        for at in chunks:
            a_v[at, :] = l_row[slot, at, :].astype(F32)
        products(t, a_v, lambda p, k: p * t + k, b_v, lambda k: pl.ds(k, t, stride=t), own_v, True)

    def forward_step(s, _):
        forward(10, l_row, s)
        both(s, share)

        @pl.when(s == 1)
        def _():
            combine(col)

        @pl.when(s > 1)
        def _():
            both(s - 1, combine)

        return 0

    lax.fori_loop(1, peers, forward_step, 0)

    @pl.when(row != col)
    def _():
        start_rest()

    def send_l(s, _):
        left_over_rows(row, lax.rem(row + s, peers)).start()
        return 0

    lax.fori_loop(1, peers, send_l, 0)
    both(peers - 1, combine)

    for n, at in enumerate(chunks):
        hat, inv = ln(own_v[at, :])
        mixed = (hat * gmid_ref[...]).astype(BF16)
        out = nn(mixed, wout_ref[...])
        gate = proj_v[at, 4 * c :]
        carried = (x_ref[at, :].astype(F32) + gate * out).astype(BF16).astype(F32)
        hat_t, inv_t = ln(carried)
        up = nn((hat_t * gtr_ref[...]).astype(BF16), wup_ref[...])
        hidden = jnp.maximum(up, 0.0).astype(BF16)
        up_ref[at, :] = (carried + nn(hidden, wdn_ref[...])).astype(BF16)
        cot = cot_ref[at, :]
        d_hidden = nt(cot, wdn_ref[...]).astype(BF16)
        d_up = jnp.where(up > 0.0, d_hidden.astype(F32), 0.0).astype(BF16)
        d_lifted = nt(d_up, wup_ref[...]).astype(BF16).astype(F32)
        d_car = cot.astype(F32) + ln_back(d_lifted * gtr_ref[...], hat_t, inv_t)
        dcar_v[at, :] = d_car
        dgate_v[at, :] = d_car * out * gate * (1.0 - gate)
        d_mixed = nt((d_car * gate).astype(BF16), wout_ref[...]).astype(BF16).astype(F32)
        dc_row[col, at, :] = ln_back(d_mixed * gmid_ref[...], hat, inv).astype(BF16)

        for up in (True, False):
            pass_on(13, dc_row, col, n, up)
        dleft_v[at, :] = jnp.zeros((step, c), F32)
        dright_v[at, :] = jnp.zeros((step, c), F32)

    def hand_on(tile):
        @pl.when(tile == row)
        def _():
            dc_col[row] = dc_row[tile]

        @pl.when(tile != row)
        def _():
            dc_over_rows(tile, row, tile).start()

    def to_left(tile):
        @pl.when((tile != row) & (tile != col))
        def _():
            wait_rest(tile)

        for at in chunks:
            a_v[at, :] = dc_row[tile, at, :].astype(F32)
            b_v[at, :] = r_all[tile, at, :].astype(F32)
        products(t, a_v, lambda p, j: p * t + j, b_v, lambda j: pl.ds(j * t, t), dleft_v, True)

    hand_on(col)

    def back_step(s, _):
        forward(13, dc_row, s)
        both(s, hand_on)

        @pl.when(s == 1)
        def _():
            to_left(col)

        @pl.when(s > 1)
        def _():
            both(s - 1, to_left)

        return 0

    lax.fori_loop(1, peers, back_step, 0)
    both(peers - 1, to_left)

    def right_step(s, _):
        src = lax.rem(row - s + peers, peers)

        @pl.when(s > 0)
        def _():
            left_over_rows(src, src).wait_recv()
            dc_over_rows(src, src, src).wait_recv()

        for at in chunks:
            a_v[at, :] = dc_col[src, at, :].astype(F32)
            b_v[at, :] = l_all[src, at, :].astype(F32)
        products(t, a_v, lambda p, i: i * t + p, b_v, lambda i: pl.ds(i * t, t), dright_v, True)
        return 0

    lax.fori_loop(0, peers, right_step, 0)

    for at in chunks:
        total = None
        for n, d_ref in ((0, dleft_v), (2 * c, dright_v)):
            value, gate = proj_v[at, n : n + c], proj_v[at, n + c : n + 2 * c]
            d = d_ref[at, :] * mask_v[at, :] * gate
            d_value = d.astype(BF16)
            d_gate = (d * value * (1.0 - gate)).astype(BF16)
            term = nt(d_value, win_ref[:, n : n + c]) + nt(d_gate, win_ref[:, n + c : n + 2 * c])
            total = term if total is None else total + term
        total = total + nt(dgate_v[at, :].astype(BF16), win_ref[:, 4 * c :])
        d_normed = total.astype(BF16).astype(F32)
        d_entry = ln_back(d_normed * gin_ref[...], hat_v[at, :], inv_v[at, :])
        grad_ref[at, :] = (d_entry + dcar_v[at, :]).astype(BF16)

    def finish(tile, _):
        @pl.when(tile != row)
        def _():
            first(row, tile, mine).wait_send()
            left_over_rows(row, tile).wait_send()
            for m in range(1, PIECES):
                rest(row, m, mine, tile).wait_send()
            dc_over_rows(tile, row, tile).wait_send()

        @pl.when(tile != col)
        def _():
            to_column(tile, col, tile).wait_send()
            for m in range(1, PIECES):
                in_set(tile, m, mine, base + lax.rem(mine + m, PIECES)).wait_send()

        for kind, ref in ((10, l_row), (13, dc_row)):
            for n in range(len(chunks)):

                @pl.when((tile <= col) & (col + 1 < peers))
                def _():
                    along(kind, ref, tile, n, True).wait_send()

                @pl.when((tile >= col) & (col > 0))
                def _():
                    along(kind, ref, tile, n, False).wait_send()

        return 0

    lax.fori_loop(0, peers, finish, 0)


def shards(
    peers, pair_map, cotangent, residue_mask, gain_in, w_in, gain_mid, w_out, gain_trans, w_up, w_down
):
    t, _, c = pair_map.shape
    rows = t * t
    step = rows // 3
    tile, tile_all = (rows, c), (peers, rows, c)
    vmem = pl.BlockSpec(memory_space=pltpu.VMEM)
    up, grad = pl.pallas_call(
        functools.partial(kernel, peers, t, step),
        out_shape=[jax.ShapeDtypeStruct(tile, BF16)] * 2,
        in_specs=[pl.BlockSpec(memory_space=pltpu.SMEM)] + [vmem] * 9,
        out_specs=[vmem] * 2,
        scratch_shapes=[pltpu.VMEM(tile_all, BF16)] * 6
        + [pltpu.VMEM(tile, F32)] * 3
        + [pltpu.VMEM((rows, w_in.shape[1]), F32)]
        + [pltpu.VMEM(tile, F32)] * 7
        + [
            pltpu.SemaphoreType.DMA((22, peers)),
            pltpu.SemaphoreType.DMA((16, peers)),
        ],
        compiler_params=pltpu.CompilerParams(
            collective_id=0, has_side_effects=True, vmem_limit_bytes=48 * 1024 * 1024
        ),
    )(
        residue_mask, pair_map.reshape(tile), cotangent.reshape(tile), gain_in[None], w_in,
        gain_mid[None], w_out, gain_trans[None], w_up, w_down,
    )
    return up.reshape(pair_map.shape), grad.reshape(pair_map.shape)


def solution(mesh):
    tiles = P(("groups", "row"), "col", None)
    in_specs = (tiles, tiles, P("groups")) + (P(),) * 7
    return jax.shard_map(
        functools.partial(shards, mesh.shape["row"]),
        mesh=mesh, in_specs=in_specs, out_specs=(tiles, tiles), check_vma=False,
    )
```

```python
import functools

import jax
import jax.numpy as jnp
from jax import lax
from jax.experimental import pallas as pl
from jax.experimental.pallas import tpu as pltpu
from jax.sharding import PartitionSpec as P

epsilon = 1e-05
PIECES = 4
MESH = pl.DeviceIdType.MESH
F32 = jnp.float32
BF16 = jnp.bfloat16


def nn(a, b):
    return jnp.dot(a, b, preferred_element_type=F32)


def nt(a, b):
    return lax.dot_general(a, b, (((1,), (1,)), ((), ())), preferred_element_type=F32)


def ln(values):
    centred = values - jnp.mean(values, axis=-1, keepdims=True)
    inv = lax.rsqrt(jnp.mean(centred * centred, axis=-1, keepdims=True) + epsilon)
    return centred * inv, inv


def ln_back(d_hat, hat, inv):
    return inv * (
        d_hat
        - jnp.mean(d_hat, axis=-1, keepdims=True)
        - hat * jnp.mean(d_hat * hat, axis=-1, keepdims=True)
    )


def sigmoid(v):
    return jax.nn.sigmoid(v)


def products(t, a_ref, a_row, b_ref, b_rows, out_ref, add):
    def block(n, _):
        acc = [None] * 8
        for s in range(t):
            b = b_ref[b_rows(s), :]
            for u in range(8):
                term = a_ref[pl.ds(a_row(n * 8 + u, s), 1), :] * b
                acc[u] = term if acc[u] is None else acc[u] + term
        for u in range(8):
            at = pl.ds(pl.multiple_of((n * 8 + u) * t, 8), t)
            out_ref[at, :] = out_ref[at, :] + acc[u] if add else acc[u]
        return 0

    lax.fori_loop(0, t // 8, block, 0)


def kernel(
    peers, t, step,
    mask_hbm, x_hbm, cot_hbm, gin_hbm, win_hbm, gmid_hbm, wout_hbm, gtr_hbm, wup_hbm, wdn_hbm,
    up_ref, grad_ref,
    mask_ref, x_ref, cot_ref, gin_ref, win_ref, gmid_ref, wout_ref, gtr_ref, wup_ref, wdn_ref, in_sem,
    r_all, l_all, rt, l_row, dc_row, dc_col,
    mask_v, hat_v, inv_v, proj_v, own_v, a_v, b_v, dleft_v, dright_v, dcar_v, dgate_v,
    s_send, s_recv,
):
    row, col = lax.axis_index("row"), lax.axis_index("col")
    rows = t * t
    c = x_ref.shape[-1]
    chunks = [pl.ds(n, step) for n in range(0, rows, step)]

    barrier = pltpu.get_barrier_semaphore()
    for s in range(1, peers):
        pl.semaphore_signal(
            barrier, inc=1, device_id={"row": lax.rem(row + s, peers)}, device_id_type=MESH
        )
        pl.semaphore_signal(
            barrier, inc=1, device_id={"col": lax.rem(col + s, peers)}, device_id_type=MESH
        )

    ins = [
        pltpu.make_async_copy(src, dst, in_sem.at[n])
        for n, (src, dst) in enumerate((
            (mask_hbm, mask_ref), (x_hbm, x_ref), (gin_hbm, gin_ref), (win_hbm, win_ref),
            (cot_hbm, cot_ref), (gmid_hbm, gmid_ref), (wout_hbm, wout_ref), (gtr_hbm, gtr_ref),
            (wup_hbm, wup_ref), (wdn_hbm, wdn_ref),
        ))
    ]
    for load in ins:
        load.start()

    def copy(kind, src, dst, slot, axis, peer, lane=None):
        return pltpu.make_async_remote_copy(
            src_ref=src, dst_ref=dst,
            send_sem=s_send.at[kind if lane is None else lane, peer if lane is None else slot],
            recv_sem=s_recv.at[kind, slot], device_id={axis: peer}, device_id_type=MESH,
        )

    size = rows // PIECES
    mine = lax.rem(row, PIECES)
    base = row - mine

    def part(ref, slot, p):
        return ref.at[slot, pl.ds(pl.multiple_of(p * size, 16), size)]

    def first(src, peer, p):
        return copy(0, part(r_all, src, p), part(r_all, src, p), src, "row", peer)

    def left_over_rows(src, peer):
        return copy(1, l_all.at[src], l_all.at[src], src, "row", peer)

    def to_column(src, slot, peer):
        return copy(2, part(r_all, src, mine), part(rt, slot, mine), slot, "col", peer)

    def in_set(slot, m, p, peer):
        d = part(rt, slot, p)
        return copy(2 + m, d, d, slot, "row", peer, lane=2 + m)

    def rest(src, m, p, peer):
        d = part(r_all, src, p)
        return copy(5 + m, d, d, src, "row", peer)

    def dc_over_rows(src, slot, peer, n):
        return copy(16 + n, dc_row.at[src, chunks[n]], dc_col.at[slot, chunks[n]], slot, "row", peer)

    def along(kind, ref, tile, n, up):
        d = ref.at[tile, chunks[n]]
        peer = col + 1 if up else col - 1
        return copy(kind + n, d, d, tile, "col", peer, lane=kind + n + (0 if up else 9))

    def pass_on(kind, ref, tile, n, up):
        @pl.when((col + 1 < peers) if up else (col > 0))
        def _():
            along(kind, ref, tile, n, up).start()

    def forward(kind, ref, s, then=None):
        for n in range(len(chunks)):
            for up in (True, False):
                tile = col - s if up else col + s

                @pl.when((tile >= 0) if up else (tile < peers))
                def _():
                    along(kind, ref, tile, n, not up).wait_recv()
                    pass_on(kind, ref, tile, n, up)
                    if then is not None:
                        then(tile, n)

    def both(s, body):
        @pl.when(col - s >= 0)
        def _():
            body(col - s)

        @pl.when(col + s < peers)
        def _():
            body(col + s)

    def start_rest():
        def per_peer(s, _):
            peer = lax.rem(row + s, peers)
            for m in range(1, PIECES):
                rest(row, m, lax.rem(lax.rem(peer, PIECES) + m, PIECES), peer).start()
            return 0

        lax.fori_loop(1, peers, per_peer, 0)

    def wait_rest(src):
        for m in range(1, PIECES):
            rest(src, m, lax.rem(mine + m, PIECES), src).wait_recv()

    for load in ins[:4]:
        load.wait()

    at_k = lax.broadcasted_iota(jnp.int32, (t, c), 0)
    m_k = jnp.zeros((t, c), F32)
    for k in range(t):
        m_k = jnp.where(at_k == k, mask_ref[col * t + k].astype(F32), m_k)
    for i in range(t):
        mask_v[i * t : (i + 1) * t, :] = m_k * mask_ref[row * t + i].astype(F32)

    for at in chunks:
        hat, inv = ln(x_ref[at, :].astype(F32))
        hat_v[at, :] = hat
        inv_v[at, :] = jnp.broadcast_to(inv, hat.shape)
        normed = (hat * gin_ref[...]).astype(BF16)
        pr = nn(normed, win_ref[:, 2 * c : 4 * c])
        gate = sigmoid(pr[:, c:])
        proj_v[at, 2 * c : 3 * c] = pr[:, :c]
        proj_v[at, 3 * c : 4 * c] = gate
        r_all[row, at, :] = (mask_v[at, :] * gate * pr[:, :c]).astype(BF16)

    for n, at in enumerate(chunks):
        normed = (hat_v[at, :] * gin_ref[...]).astype(BF16)
        pr = nn(normed, win_ref[:, : 2 * c])
        gate = sigmoid(pr[:, c:])
        proj_v[at, :c] = pr[:, :c]
        proj_v[at, c : 2 * c] = gate
        left = (mask_v[at, :] * gate * pr[:, :c]).astype(BF16)
        l_row[col, at, :] = left
        l_all[row, at, :] = left

    pl.semaphore_wait(barrier, 2 * (peers - 1))

    def send_r(s, _):
        peer = lax.rem(row + s, peers)
        first(row, peer, lax.rem(peer, PIECES)).start()
        return 0

    lax.fori_loop(1, peers, send_r, 0)

    for n in range(len(chunks)):
        for up in (True, False):
            pass_on(10, l_row, col, n, up)

    def piece_step(s, _):
        src = lax.rem(row - s + peers, peers)

        @pl.when(s > 0)
        def _():
            first(src, src, mine).wait_recv()

        @pl.when(src != col)
        def _():
            to_column(src, col, src).start()

        return 0

    lax.fori_loop(0, peers, piece_step, 0)

    @pl.when(row == col)
    def _():
        start_rest()

    for at in chunks:
        normed = (hat_v[at, :] * gin_ref[...]).astype(BF16)
        proj_v[at, 4 * c :] = sigmoid(nn(normed, win_ref[:, 4 * c :]))
        own_v[at, :] = jnp.zeros((step, c), F32)

    def share(slot):
        to_column(slot, slot, slot).wait_recv()
        for m in range(1, PIECES):
            in_set(slot, m, mine, base + lax.rem(mine + m, PIECES)).start()

    def combine(slot):
        @pl.when(slot == col)
        def _():
            @pl.when(row != col)
            def _():
                wait_rest(col)

            for at in chunks:
                b_v[at, :] = r_all[col, at, :].astype(F32)

        @pl.when(slot != col)
        def _():
            for m in range(1, PIECES):
                p = lax.rem(mine - m + PIECES, PIECES)
                in_set(slot, m, p, base + p).wait_recv()
            for at in chunks:
                b_v[at, :] = rt[slot, at, :].astype(F32)

        for at in chunks:
            a_v[at, :] = l_row[slot, at, :].astype(F32)
        products(t, a_v, lambda p, k: p * t + k, b_v, lambda k: pl.ds(k, t, stride=t), own_v, True)

    def send_l(s, _):
        left_over_rows(row, lax.rem(row + s, peers)).start()
        return 0

    def forward_step(s, _):
        forward(10, l_row, s)

        @pl.when(s == 1)
        def _():
            def share_step(d, _):
                both(d, share)
                return 0

            lax.fori_loop(1, peers, share_step, 0)

            @pl.when(row != col)
            def _():
                start_rest()

            lax.fori_loop(1, peers, send_l, 0)
            combine(col)

        @pl.when(s > 1)
        def _():
            both(s - 1, combine)

        return 0

    lax.fori_loop(1, peers, forward_step, 0)
    both(peers - 1, combine)

    for load in ins[4:]:
        load.wait()

    for n, at in enumerate(chunks):
        hat, inv = ln(own_v[at, :])
        mixed = (hat * gmid_ref[...]).astype(BF16)
        out = nn(mixed, wout_ref[...])
        gate = proj_v[at, 4 * c :]
        carried = (x_ref[at, :].astype(F32) + gate * out).astype(BF16).astype(F32)
        hat_t, inv_t = ln(carried)
        up = nn((hat_t * gtr_ref[...]).astype(BF16), wup_ref[...])
        hidden = jnp.maximum(up, 0.0).astype(BF16)
        up_ref[at, :] = (carried + nn(hidden, wdn_ref[...])).astype(BF16)
        cot = cot_ref[at, :]
        d_hidden = nt(cot, wdn_ref[...]).astype(BF16)
        d_up = jnp.where(up > 0.0, d_hidden.astype(F32), 0.0).astype(BF16)
        d_lifted = nt(d_up, wup_ref[...]).astype(BF16).astype(F32)
        d_car = cot.astype(F32) + ln_back(d_lifted * gtr_ref[...], hat_t, inv_t)
        dcar_v[at, :] = d_car
        dgate_v[at, :] = d_car * out * gate * (1.0 - gate)
        d_mixed = nt((d_car * gate).astype(BF16), wout_ref[...]).astype(BF16).astype(F32)
        dc_row[col, at, :] = ln_back(d_mixed * gmid_ref[...], hat, inv).astype(BF16)

        for up in (True, False):
            pass_on(13, dc_row, col, n, up)
        dleft_v[at, :] = jnp.zeros((step, c), F32)
        dright_v[at, :] = jnp.zeros((step, c), F32)

    def hand_on(tile, n):
        @pl.when(tile == row)
        def _():
            dc_col[row, chunks[n], :] = dc_row[tile, chunks[n], :]

        @pl.when(tile != row)
        def _():
            dc_over_rows(tile, row, tile, n).start()

    def to_left(tile):
        @pl.when((tile != row) & (tile != col))
        def _():
            wait_rest(tile)

        for at in chunks:
            a_v[at, :] = dc_row[tile, at, :].astype(F32)
            b_v[at, :] = r_all[tile, at, :].astype(F32)
        products(t, a_v, lambda p, j: p * t + j, b_v, lambda j: pl.ds(j * t, t), dleft_v, True)

    for n in range(len(chunks)):
        hand_on(col, n)

    def right_step(s, _):
        src = lax.rem(row - s + peers, peers)

        @pl.when(s > 0)
        def _():
            left_over_rows(src, src).wait_recv()
            for n in range(len(chunks)):
                dc_over_rows(src, src, src, n).wait_recv()

        for at in chunks:
            a_v[at, :] = dc_col[src, at, :].astype(F32)
            b_v[at, :] = l_all[src, at, :].astype(F32)
        products(t, a_v, lambda p, i: i * t + p, b_v, lambda i: pl.ds(i * t, t), dright_v, True)
        return 0

    def back_step(s, _):
        forward(13, dc_row, s, hand_on)

        @pl.when(s == 1)
        def _():
            to_left(col)

        @pl.when(s > 1)
        def _():
            both(s - 1, to_left)

        return 0

    lax.fori_loop(1, peers, back_step, 0)
    both(peers - 1, to_left)
    lax.fori_loop(0, peers, right_step, 0)


    for at in chunks:
        total = None
        for n, d_ref in ((0, dleft_v), (2 * c, dright_v)):
            value, gate = proj_v[at, n : n + c], proj_v[at, n + c : n + 2 * c]
            d = d_ref[at, :] * mask_v[at, :] * gate
            d_value = d.astype(BF16)
            d_gate = (d * value * (1.0 - gate)).astype(BF16)
            term = nt(d_value, win_ref[:, n : n + c]) + nt(d_gate, win_ref[:, n + c : n + 2 * c])
            total = term if total is None else total + term
        total = total + nt(dgate_v[at, :].astype(BF16), win_ref[:, 4 * c :])
        d_normed = total.astype(BF16).astype(F32)
        d_entry = ln_back(d_normed * gin_ref[...], hat_v[at, :], inv_v[at, :])
        grad_ref[at, :] = (d_entry + dcar_v[at, :]).astype(BF16)

    def finish(tile, _):
        @pl.when(tile != row)
        def _():
            first(row, tile, mine).wait_send()
            left_over_rows(row, tile).wait_send()
            for m in range(1, PIECES):
                rest(row, m, mine, tile).wait_send()
            for n in range(len(chunks)):
                dc_over_rows(tile, row, tile, n).wait_send()

        @pl.when(tile != col)
        def _():
            to_column(tile, col, tile).wait_send()
            for m in range(1, PIECES):
                in_set(tile, m, mine, base + lax.rem(mine + m, PIECES)).wait_send()

        for kind, ref in ((10, l_row), (13, dc_row)):
            for n in range(len(chunks)):

                @pl.when((tile <= col) & (col + 1 < peers))
                def _():
                    along(kind, ref, tile, n, True).wait_send()

                @pl.when((tile >= col) & (col > 0))
                def _():
                    along(kind, ref, tile, n, False).wait_send()

        return 0

    lax.fori_loop(0, peers, finish, 0)


def shards(
    peers, pair_map, cotangent, residue_mask, gain_in, w_in, gain_mid, w_out, gain_trans, w_up, w_down
):
    t, _, c = pair_map.shape
    rows = t * t
    step = rows // 3
    tile, tile_all = (rows, c), (peers, rows, c)
    args = (
        residue_mask, pair_map.reshape(tile), cotangent.reshape(tile), gain_in[None], w_in,
        gain_mid[None], w_out, gain_trans[None], w_up, w_down,
    )
    vmem = pl.BlockSpec(memory_space=pltpu.VMEM)
    up, grad = pl.pallas_call(
        functools.partial(kernel, peers, t, step),
        out_shape=[jax.ShapeDtypeStruct(tile, BF16)] * 2,
        in_specs=[pl.BlockSpec(memory_space=pltpu.HBM)] * 10,
        out_specs=[vmem] * 2,
        scratch_shapes=[pltpu.SMEM(args[0].shape, jnp.int32)]
        + [pltpu.VMEM(a.shape, a.dtype) for a in args[1:]]
        + [pltpu.SemaphoreType.DMA((len(args),))]
        + [pltpu.VMEM(tile_all, BF16)] * 6
        + [pltpu.VMEM(tile, F32)] * 3
        + [pltpu.VMEM((rows, w_in.shape[1]), F32)]
        + [pltpu.VMEM(tile, F32)] * 7
        + [
            pltpu.SemaphoreType.DMA((25, peers)),
            pltpu.SemaphoreType.DMA((19, peers)),
        ],
        compiler_params=pltpu.CompilerParams(
            collective_id=0, has_side_effects=True, vmem_limit_bytes=63 * 1024 * 1024
        ),
    )(*args)
    return up.reshape(pair_map.shape), grad.reshape(pair_map.shape)


def solution(mesh):
    tiles = P(("groups", "row"), "col", None)
    in_specs = (tiles, tiles, P("groups")) + (P(),) * 7
    return jax.shard_map(
        functools.partial(shards, mesh.shape["row"]),
        mesh=mesh, in_specs=in_specs, out_specs=(tiles, tiles), check_vma=False,
    )
```
